256 devices in a mesh: cfg: 2 (over x_lo), patch: 16 (over x_hi, y, core), head: 8 (over z).
Axes of the slice: x: 4 (x_hi: 2, x_lo: 2; x = x_hi * 2 + x_lo), y: 4, z: 8, core: 2. Of those that a mesh axis runs over, the one named last changes fastest.
Arguments:
- hidden_states: bfloat16 [2, 6144, 5120], P('cfg', 'patch'), may hold values from -6 to 6
- modulation: float32 [2, 5120], replicated, may hold values from -3 to 3
- w_query: bfloat16 [5120, 5120], P('cfg', 'head')
- w_key: bfloat16 [5120, 5120], P('cfg', 'head')
- w_value: bfloat16 [5120, 5120], P('cfg', 'head'), may hold values from -0.078125 to 0.078125
- query_gain: float32 [5120], P('head'), may hold values from 0.25 to 1.75
- key_gain: float32 [5120], P('head'), may hold values from 0.25 to 1.75
- stale_kv: bfloat16 [2, 2, 6144, 5120], P('cfg', None, 'patch', 'head'), may hold values from -6 to 6
Outputs:
- attended: bfloat16 [2, 6144, 5120], P('cfg', 'patch', 'head')
- fresh_kv: bfloat16 [2, 2, 6144, 5120], P('cfg', None, 'patch', 'head')
The draws below stay inside these ranges and needn't reach their ends.
All inputs are finite; a program needn't handle non-finite values.
Results may differ from the reference program's by a relative error of at most 0.008.
Values may be sent and summed in bfloat16 or wider, within the bound.
A program may use at most 192 MiB of HBM per device.

```python
import jax
import jax.numpy as jnp
from jax import lax

D = 5120
HEADS = 40
HEAD_DIM = 128
TOK_DEV = 384
TOKENS = 6144
N_PATCH = 16


def shared_base(key):
    return jax.random.normal(key, (D, HEADS * HEAD_DIM), jnp.float32)


def column_ramp(power):
    column = jnp.arange(HEADS * HEAD_DIM, dtype=jnp.float32)
    return (1.0 + 2.0 * column / (HEADS * HEAD_DIM - 1.0)) ** power


def draw_w_query(key, part):
    base = shared_base(key)
    values = base * column_ramp(0.5)
    return (values / jnp.sqrt(jnp.float32(D))).astype(jnp.bfloat16)


def draw_w_key(key, part):
    key = jax.random.fold_in(key, 23)
    own = jax.random.normal(key, (D, HEADS * HEAD_DIM), jnp.float32)
    values = own * column_ramp(0.5)
    return (values / jnp.sqrt(jnp.float32(D))).astype(jnp.bfloat16)


def draw_stale_kv(key, part):
    key = jax.random.fold_in(key, 37)
    noise_key = jax.random.fold_in(key, 0)
    noise = jax.random.normal(noise_key, (2, 2, TOKENS, HEADS * HEAD_DIM), jnp.float32)
    values = noise
    return jnp.clip(values, -6.0, 6.0).astype(jnp.bfloat16)


def steps_of(stream_key, dims, pieces, smallest, largest):
    def one(axis_at, parts):
        draws = jax.random.uniform(jax.random.fold_in(jax.random.fold_in(stream_key, 6), axis_at), (parts,), jnp.float32, smallest / len(pieces), largest / len(pieces))
        return jnp.repeat(jnp.exp(draws), dims[axis_at] // parts).reshape((-1,) + (1,) * (len(dims) - axis_at - 1))

    level = one(*pieces[0])
    for cut in pieces[1:]:
        level = level * one(*cut)
    return level


def centred(stream_key, extent, scale, limit, shards=(), held_as=jnp.bfloat16):
    drawn = scale * jax.random.normal(stream_key, extent, jnp.float32)
    if shards:
        drawn = drawn * steps_of(stream_key, extent, shards, -0.22, 0.18)
    return jnp.clip(drawn, -limit, limit).astype(held_as)


def setup_inputs(seed: int = 0) -> dict:
    key_list = jax.random.split(jax.random.key(seed), 9)
    return {
        "hidden_states": centred(key_list[0], (2, TOKENS, D), 1.0, 6.0, ((0, 2), (1, 16))),
        "modulation": centred(key_list[1], (2, D), 0.5, 3.0, (), jnp.float32),
        "w_query": draw_w_query(jax.random.fold_in(key_list[8], 71), 0),
        "w_key": draw_w_key(jax.random.fold_in(key_list[8], 71), 0),
        "w_value": centred(key_list[4], (D, HEADS * HEAD_DIM), D ** -0.5, 0.078125, ((0, 2), (1, 8))),
        "query_gain": jnp.clip(1.0 + 0.15 * jax.random.normal(key_list[5], (HEADS * HEAD_DIM,), jnp.float32), 0.25, 1.75),
        "key_gain": jnp.clip(1.0 + 0.15 * jax.random.normal(key_list[6], (HEADS * HEAD_DIM,), jnp.float32), 0.25, 1.75),
        "stale_kv": draw_stale_kv(jax.random.fold_in(key_list[8], 71), 0),
    }


def rms_scale(raw, gain):
    stat = lax.optimization_barrier(jnp.mean(raw * raw, axis=-1, keepdims=True))
    return (raw * lax.rsqrt(stat + 1e-06) * gain).astype(jnp.bfloat16)

def reference(hidden_states, modulation, w_query, w_key, w_value, query_gain, key_gain, stale_kv):
    states = hidden_states.astype(jnp.float32)
    mean = lax.optimization_barrier(jnp.mean(states, axis=-1, keepdims=True))
    var = lax.optimization_barrier(jnp.mean((states - mean) ** 2, axis=-1, keepdims=True))
    normed = ((states - mean) * lax.rsqrt(var + 1e-06) * (1.0 + modulation[1]) + modulation[0]).astype(jnp.bfloat16)
    flat = normed.reshape(2 * TOKENS, D)
    query = rms_scale(jnp.dot(flat, w_query, preferred_element_type=jnp.float32), query_gain)
    key = rms_scale(jnp.dot(flat, w_key, preferred_element_type=jnp.float32), key_gain)
    value = jnp.dot(flat, w_value, preferred_element_type=jnp.float32).astype(jnp.bfloat16)
    query = query.reshape(2, TOKENS, HEADS * HEAD_DIM)
    key = key.reshape(2, TOKENS, HEADS * HEAD_DIM)
    value = value.reshape(2, TOKENS, HEADS * HEAD_DIM)
    fresh_kv = jnp.stack([key, value], axis=1)

    def one_block(number):
        branch = (number // N_PATCH).astype(jnp.int32)
        block = (number % N_PATCH).astype(jnp.int32)
        begin = (block * TOK_DEV).astype(jnp.int32)
        fresh_b = lax.dynamic_index_in_dim(fresh_kv, branch, 0, keepdims=False)
        stale_b = lax.dynamic_index_in_dim(stale_kv, branch, 0, keepdims=False)
        own = lax.dynamic_slice_in_dim(fresh_b, begin, TOK_DEV, 1)
        mixed = lax.dynamic_update_slice_in_dim(stale_b, own, begin, 1)
        rows = lax.dynamic_slice_in_dim(lax.dynamic_index_in_dim(query, branch, 0, keepdims=False), begin, TOK_DEV, 0)
        qh = rows.reshape(TOK_DEV, HEADS, HEAD_DIM).astype(jnp.float32)
        kh = mixed[0].reshape(TOKENS, HEADS, HEAD_DIM).astype(jnp.float32)
        vh = mixed[1].reshape(TOKENS, HEADS, HEAD_DIM).astype(jnp.float32)
        score = jnp.einsum('qhd,khd->hqk', qh, kh) / jnp.sqrt(jnp.float32(HEAD_DIM))
        top = lax.optimization_barrier(jnp.max(score, axis=-1, keepdims=True))
        expo = jnp.exp(score - top)
        total = lax.optimization_barrier(jnp.sum(expo, axis=-1))
        weight = expo.astype(jnp.bfloat16).astype(jnp.float32)
        summed = jnp.einsum('hqk,khd->qhd', weight, vh)
        result = summed / jnp.transpose(total)[:, :, None]
        return result.reshape(TOK_DEV, HEADS * HEAD_DIM).astype(jnp.bfloat16)
    numbers = jnp.arange(2 * N_PATCH, dtype=jnp.int32)
    attended = lax.map(one_block, numbers).reshape(2, TOKENS, HEADS * HEAD_DIM)
    return (attended, fresh_kv)
```

```python
import functools

import jax
import jax.numpy as jnp
from jax import lax
from jax.experimental import pallas as pl
from jax.experimental.pallas import tpu as pltpu
from jax.sharding import PartitionSpec as P

HEAD_DIM = 128
SCORE_SCALE = 1.4426950408889634 / 128.0**0.5
LOW = -1e30
MESH = pl.DeviceIdType.MESH
F32 = jnp.float32
BF16 = jnp.bfloat16


def kernel(
    n_head, columns_all,
    hid_any, mod, wq_any, wk_any, wv_any, gain_q, gain_k, stale_any,
    att_out, fresh,
    hid, nrm, wown, woth, raw, kvs, qs, top, acc, o_send, o_recv, lse_send, lse_recv, zs,
    ld, wps, wpr, wss, wsr, kys, kyr, k3s, k3r, kss, ksr, qss, qsr, oss, osr, zss, zsr,
):
    tok = hid.shape[0]
    depth = wown.shape[1]
    width = wown.shape[2]
    heads = width // HEAD_DIM
    quarter = depth // 4
    part = quarter // 2
    half = tok // 2

    c = lax.axis_index("cfg")
    p = lax.axis_index("patch")
    h = lax.axis_index("head")
    core = p % 2
    y = (p // 2) % 4
    xh = p // 8

    def at(xh_, y_, core_):
        return (xh_ * 4 + y_) * 2 + core_

    SIB = (c, at(xh, y, 1 - core), h)
    XD = (1 - c, p, h)
    XO = (1 - c, at(1 - xh, y, core), h)
    X2 = (c, at(1 - xh, y, core), h)
    YP = (c, at(xh, (y + 1) % 4, core), h)
    YM = (c, at(xh, (y + 3) % 4, core), h)
    ZS = [(c, p, (h + d) % n_head) for d in range(1, n_head)]
    w_any = (wq_any, wk_any, wv_any)

    loads = [
        pltpu.make_async_copy(hid_any.at[0], hid, ld.at[0]),
        pltpu.make_async_copy(wq_any, wown.at[0], ld.at[1]),
        pltpu.make_async_copy(wk_any, wown.at[1], ld.at[2]),
        pltpu.make_async_copy(wv_any, wown.at[2], ld.at[3]),
        pltpu.make_async_copy(stale_any.at[0], kvs.at[0, :, pl.ds(0, tok)], ld.at[4]),
    ]

    barrier = pltpu.get_barrier_semaphore()
    partners = [SIB, XD, XO, X2, YP, YM] + ZS
    for device in partners:
        pl.semaphore_signal(barrier, inc=1, device_id=device, device_id_type=MESH)
    for load in loads:
        load.start()
    pl.semaphore_wait(barrier, len(partners))

    sent = []

    def send(src, dst, ss, rs, device):
        copy = pltpu.make_async_remote_copy(
            src_ref=src, dst_ref=dst, send_sem=ss, recv_sem=rs, device_id=device, device_id_type=MESH
        )
        copy.start()
        return copy

    def pending(describe):
        sent.append(describe)

    def arrived(dst, rs):
        pltpu.make_async_remote_copy(
            src_ref=dst, dst_ref=dst, send_sem=rs, recv_sem=rs, device_id=SIB, device_id_type=MESH
        ).wait_recv()

    def quarter_of(d):
        return (y + d) % 4

    def piece(d, side):
        return pl.ds(pl.multiple_of(quarter_of(d) * quarter + side * part, 16), part)

    def whole(d):
        return pl.ds(pl.multiple_of(quarter_of(d) * quarter, 16), quarter)

    def weight_x(m, d, device):
        rows = piece(d, core)
        send(w_any[m].at[rows], woth.at[m, rows], wps.at[m, d], wpr.at[m, d], device)
        pending(lambda: (w_any[m].at[piece(d, core)], wps.at[m, d]))

    def weight_sib(m, d):
        rows = piece(d, core)
        arrived(woth.at[m, rows], wpr.at[m, d])
        send(woth.at[m, rows], woth.at[m, rows], wss.at[m, d], wsr.at[m, d], SIB)
        pending(lambda: (woth.at[m, piece(d, core)], wss.at[m, d]))

    def weight_y(m):
        rows = piece(0, core)
        for d, device in ((3, YP), (1, YM)):
            send(woth.at[m, rows], woth.at[m, rows], wps.at[m, d], wpr.at[m, d], device)
            pending(lambda d=d: (woth.at[m, piece(0, core)], wps.at[m, d]))

    def weight_dot(m, d):
        arrived(woth.at[m, piece(d, 1 - core)], wsr.at[m, d])
        lanes = pl.ds(pl.multiple_of((1 - c) * depth + quarter_of(d) * quarter, 128), quarter)
        raw[m] += jnp.dot(nrm[:, lanes], woth[m, whole(d), :], preferred_element_type=F32)

    mine = pl.ds(0, tok)
    other = pl.ds(tok, tok)

    def kv_out(i):
        src = stale_any.at[0, i]
        send(src, kvs.at[2, i, mine], kys.at[0, i], kyr.at[1, i], YP)
        send(src, kvs.at[1, i, mine], kys.at[1, i], kyr.at[0, i], YM)
        send(src, kvs.at[0, i, other], kss.at[0, i], ksr.at[0, i], SIB)
        pending(lambda: (stale_any.at[0, i], kys.at[0, i]))
        pending(lambda: (stale_any.at[0, i], kys.at[1, i]))
        pending(lambda: (stale_any.at[0, i], kss.at[0, i]))

    def kv_sib(slot, i):
        send(kvs.at[slot, i, mine], kvs.at[slot, i, other], kss.at[slot, i], ksr.at[slot, i], SIB)
        pending(lambda: (kvs.at[slot, i, pl.ds(0, tok)], kss.at[slot, i]))

    def kv_forward(i):
        for k, device in ((0, YM), (1, YP)):
            rows = pl.ds(k * half, half)
            arrived(kvs.at[1 + k, i, mine], kyr.at[k, i])
            send(kvs.at[1 + k, i, rows], kvs.at[3, i, rows], k3s.at[k, i], k3r.at[k, i], device)
            pending(lambda k=k: (kvs.at[1 + k, i, pl.ds(k * half, half)], k3s.at[k, i]))
            kv_sib(1 + k, i)

    def kv_last(i):
        for k in range(2):
            arrived(kvs.at[3, i, pl.ds(k * half, half)], k3r.at[k, i])
        kv_sib(3, i)

    def kv_ready(slot):
        for i in range(2):
            arrived(kvs.at[slot, i, other], ksr.at[slot, i])

    def squares_out(k, m):
        r = raw[m]
        column = jnp.sum(r * r, axis=1, keepdims=True)
        zs[k, 0] = jnp.transpose(jnp.broadcast_to(column, (tok, 128)))[:8, :]
        for d in range(1, n_head):
            send(zs.at[k, 0], zs.at[k, d], zss.at[k, d - 1], zsr.at[k, d - 1], ZS[d - 1])
            pending(lambda d=d: (zs.at[k, 0], zss.at[k, d - 1]))

    def normalised(k, m, gain):
        total = zs[k, 0]
        for d in range(1, n_head):
            arrived(zs.at[k, d], zsr.at[k, d - 1])
            total = total + zs[k, d]
        factor = lax.rsqrt(total / columns_all + 1e-06)
        factor = jnp.transpose(jnp.broadcast_to(factor[:1, :], (128, tok)))
        return [
            (raw[m, :, j * 128 : (j + 1) * 128] * factor * gain[:, j * 128 : (j + 1) * 128]).astype(BF16)
            for j in range(heads)
        ]

    tiles = 3 if tok % 48 == 0 else 1
    step = tok // tiles

    def attend(s, key_ref, value_ref):
        for j in range(heads):
            lanes = slice(j * 128, (j + 1) * 128)
            for t in range(tiles):
                rows = slice(t * step, (t + 1) * step)
                key = key_ref[:, lanes]
                value = value_ref[:, lanes]
                score = lax.dot_general(
                    qs[s, rows, lanes], key, (((1,), (1,)), ((), ())), preferred_element_type=F32
                )
                score = score * SCORE_SCALE
                before = top[s, j, rows, :]
                now = jnp.maximum(before, jnp.max(score, axis=1, keepdims=True))
                shrink = jnp.exp2(before - now)
                weight = jnp.exp2(score - now[:, :1]).astype(BF16)
                added = jnp.dot(
                    weight, jnp.concatenate([value, jnp.ones_like(value)], axis=1), preferred_element_type=F32
                )
                acc[s, j, rows, :] = acc[s, j, rows, :] * jnp.concatenate([shrink, shrink], axis=1) + added
                top[s, j, rows, :] = now

    weight_x(0, 0, XD)
    weight_x(0, 2, XO)
    kv_out(0)

    loads[0].wait()

    def norm_rows(i, carry):
        rows = pl.ds(pl.multiple_of(i * 16, 16), 16)
        states = hid[rows, :].astype(F32)
        mean = jnp.mean(states, axis=1, keepdims=True)
        states = states - mean
        var = jnp.mean(states * states, axis=1, keepdims=True)
        nrm[rows, :] = (states * lax.rsqrt(var + 1e-06) * (1.0 + mod[1:2, :]) + mod[0:1, :]).astype(BF16)
        return carry

    lax.fori_loop(0, tok // 16, norm_rows, 0)
    weight_x(0, 1, XD)
    weight_x(0, 3, XO)
    kv_out(1)

    for load in loads[1:4]:
        load.wait()
    own_lanes = pl.ds(pl.multiple_of(c * depth, 128), depth)

    def own_dot(m, carry):
        raw[m] = jnp.dot(nrm[:, own_lanes], wown[m], preferred_element_type=F32)
        return carry

    lax.fori_loop(0, 3, own_dot, 0)

    weight_sib(0, 0)
    weight_sib(0, 2)
    kv_forward(0)
    top[...] = jnp.full_like(top, LOW)
    acc[...] = jnp.zeros_like(acc)
    weight_dot(0, 0)
    weight_dot(0, 2)
    weight_sib(0, 1)
    weight_sib(0, 3)
    weight_x(1, 0, XD)
    weight_x(1, 2, XO)
    weight_dot(0, 1)
    weight_dot(0, 3)
    squares_out(0, 0)
    kv_forward(1)
    for j, head in enumerate(normalised(0, 0, gain_q)):
        qs[0, :, j * 128 : (j + 1) * 128] = head
    send(qs.at[0], qs.at[1], qss.at[0], qsr.at[0], X2)
    pending(lambda: (qs.at[0], qss.at[0]))

    loads[4].wait()
    kv_ready(0)
    attend(0, kvs.at[0, 0, other], kvs.at[0, 1, other])

    def unit(i, carry):
        s = (i + 1) // 4
        j = (i + 1) % 4

        @pl.when(i == 0)
        def _():
            kv_ready(1)

        @pl.when(i == 1)
        def _():
            weight_sib(1, 0)
            weight_sib(1, 2)
            weight_y(1)
            weight_x(2, 0, XD)
            weight_x(2, 2, XO)
            kv_ready(2)

        @pl.when(i == 2)
        def _():
            kv_last(0)
            kv_last(1)
            kv_ready(3)

        @pl.when(i == 3)
        def _():
            arrived(qs.at[1], qsr.at[0])

        @pl.when(i == 4)
        def _():
            weight_sib(1, 1)
            weight_sib(1, 3)
            for d in (0, 2, 1, 3):
                weight_dot(1, d)
            squares_out(1, 1)

        @pl.when(i == 5)
        def _():
            weight_sib(2, 0)
            weight_sib(2, 2)
            weight_y(2)

        @pl.when(i == 6)
        def _():
            for k, head in enumerate(normalised(1, 1, gain_k)):
                fresh[0, 0, :, k * 128 : (k + 1) * 128] = head
            weight_dot(2, 0)
            weight_dot(2, 2)

        attend(s, kvs.at[j, 0], kvs.at[j, 1])
        return carry

    lax.fori_loop(0, 7, unit, 0)

    lane = lax.broadcasted_iota(jnp.int32, (tok, 128), 1)
    packed = jnp.zeros((tok, 128), F32)
    for j in range(heads):
        total = acc[1, j, :, 128:]
        o_send[:, j * 128 : (j + 1) * 128] = (acc[1, j, :, :128] / total).astype(BF16)
        packed = jnp.where(lane == j, top[1, j] + jnp.log2(total), packed)
    lse_send[...] = jnp.transpose(packed)[:8, :]
    send(lse_send, lse_recv, oss.at[1], osr.at[1], X2)
    pending(lambda: (lse_send, oss.at[1]))
    send(o_send, o_recv, oss.at[0], osr.at[0], X2)
    pending(lambda: (o_send, oss.at[0]))

    weight_sib(2, 1)
    weight_sib(2, 3)
    weight_dot(2, 1)
    weight_dot(2, 3)
    fresh[0, 1] = raw[2].astype(BF16)
    attend(0, fresh.at[0, 0], fresh.at[0, 1])

    arrived(lse_recv, osr.at[1])
    arrived(o_recv, osr.at[0])
    far = jnp.transpose(jnp.concatenate([lse_recv[...]] * 16, axis=0))
    for j in range(heads):
        lanes = slice(j * 128, (j + 1) * 128)
        near = top[0, j]
        there = jnp.broadcast_to(far[:, j : j + 1], (tok, 128))
        highest = jnp.maximum(near, there)
        a = jnp.exp2(near - highest)
        b = jnp.exp2(there - highest)
        summed = acc[0, j, :, :128] * a + o_recv[:, lanes].astype(F32) * b
        att_out[0, :, lanes] = (summed / (acc[0, j, :, 128:] * a + b)).astype(BF16)

    for describe in sent:
        src, ss = describe()
        pltpu.make_async_remote_copy(
            src_ref=src, dst_ref=src, send_sem=ss, recv_sem=ss, device_id=SIB, device_id_type=MESH
        ).wait_send()


def local(n_head, hidden_states, modulation, w_query, w_key, w_value, query_gain, key_gain, stale_kv):
    tok = hidden_states.shape[1]
    depth, width = w_query.shape
    heads = width // HEAD_DIM
    hbm = pl.BlockSpec(memory_space=pl.ANY)
    vmem = pl.BlockSpec(memory_space=pltpu.VMEM)
    dma = pltpu.SemaphoreType.DMA
    peers = max(n_head - 1, 1)
    return pl.pallas_call(
        functools.partial(kernel, n_head, float(n_head * width)),
        out_shape=(
            jax.ShapeDtypeStruct((1, tok, width), BF16),
            jax.ShapeDtypeStruct((1, 2, tok, width), BF16),
        ),
        in_specs=[hbm, vmem, hbm, hbm, hbm, vmem, vmem, hbm],
        out_specs=(vmem, vmem),
        scratch_shapes=[
            pltpu.VMEM((tok, 2 * depth), BF16),
            pltpu.VMEM((tok, 2 * depth), BF16),
            pltpu.VMEM((3, depth, width), BF16),
            pltpu.VMEM((3, depth, width), BF16),
            pltpu.VMEM((3, tok, width), F32),
            pltpu.VMEM((4, 2, 2 * tok, width), BF16),
            pltpu.VMEM((2, tok, width), BF16),
            pltpu.VMEM((2, heads, tok, 128), F32),
            pltpu.VMEM((2, heads, tok, 256), F32),
            pltpu.VMEM((tok, width), BF16),
            pltpu.VMEM((tok, width), BF16),
            pltpu.VMEM((8, tok), F32),
            pltpu.VMEM((8, tok), F32),
            pltpu.VMEM((2, n_head, 8, tok), F32),
            dma((5,)),
            dma((3, 4)), dma((3, 4)), dma((3, 4)), dma((3, 4)),
            dma((2, 2)), dma((2, 2)), dma((2, 2)), dma((2, 2)), dma((4, 2)), dma((4, 2)),
            dma((1,)), dma((1,)), dma((2,)), dma((2,)), dma((2, peers)), dma((2, peers)),
        ],
        compiler_params=pltpu.CompilerParams(
            collective_id=0, has_side_effects=True, vmem_limit_bytes=60 * 2**20
        ),
    )(
        hidden_states, modulation, w_query, w_key, w_value,
        query_gain.reshape(1, width), key_gain.reshape(1, width), stale_kv,
    )


def solution(mesh):
    in_specs = (
        P("cfg", "patch", None),
        P(),
        P("cfg", "head"),
        P("cfg", "head"),
        P("cfg", "head"),
        P("head"),
        P("head"),
        P("cfg", None, "patch", "head"),
    )
    out_specs = (P("cfg", "patch", "head"), P("cfg", None, "patch", "head"))
    run = functools.partial(local, mesh.shape["head"])
    return jax.shard_map(run, mesh=mesh, in_specs=in_specs, out_specs=out_specs, check_vma=False)
```

```python
import functools

import jax
import jax.numpy as jnp
from jax import lax
from jax.experimental import pallas as pl
from jax.experimental.pallas import tpu as pltpu
from jax.sharding import PartitionSpec as P

HEAD_DIM = 128
SCORE_SCALE = 1.4426950408889634 / 128.0**0.5
LOW = -1e30
SHARE3 = (True, False, False)
MESH = pl.DeviceIdType.MESH
F32 = jnp.float32
BF16 = jnp.bfloat16


def kernel(
    n_head, columns_all,
    hid_any, mod, wq_any, wk_any, wv_any, gain_q, gain_k, stale_any,
    att_out, fresh_out,
    att, fresh, hid, nrm, wown, woth, raw, kvs, qs, fac, fac_rows, top, acc, o_send, o_recv, lse, lse_send, lse_recv, zs,
    ld, wps, wpr, wss, wsr, kys, kyr, k3s, k3r, kss, ksr, qss, qsr, oss, osr, zss, zsr,
):
    tok = hid.shape[0]
    depth = wown.shape[1]
    width = wown.shape[2]
    heads = width // HEAD_DIM
    quarter = depth // 4
    part = quarter // 4
    half = tok // 2
    blocks = tok // 128

    c = lax.axis_index("cfg")
    p = lax.axis_index("patch")
    h = lax.axis_index("head")
    core = p % 2
    y = (p // 2) % 4
    xh = p // 8

    def at(xh_, y_, core_):
        return (xh_ * 4 + y_) * 2 + core_

    SIB = (c, at(xh, y, 1 - core), h)
    XD = (1 - c, p, h)
    XO = (1 - c, at(1 - xh, y, core), h)
    X2 = (c, at(1 - xh, y, core), h)
    YP = (c, at(xh, (y + 1) % 4, core), h)
    YM = (c, at(xh, (y + 3) % 4, core), h)
    ZS = [(c, p, (h + d) % n_head) for d in range(1, n_head)]
    w_any = (wq_any, wk_any, wv_any)

    loads = [
        pltpu.make_async_copy(hid_any.at[0], hid, ld.at[0]),
        pltpu.make_async_copy(wq_any, wown.at[0], ld.at[1]),
        pltpu.make_async_copy(wk_any, wown.at[1], ld.at[2]),
        pltpu.make_async_copy(wv_any, wown.at[2], ld.at[3]),
        pltpu.make_async_copy(stale_any.at[0], kvs.at[0, :, pl.ds(0, tok)], ld.at[4]),
    ]

    barrier = pltpu.get_barrier_semaphore()
    partners = [SIB, XD, XO, X2, YP, YM] + ZS
    for device in partners:
        pl.semaphore_signal(barrier, inc=1, device_id=device, device_id_type=MESH)
    for load in loads:
        load.start()
    pl.semaphore_wait(barrier, len(partners))

    sent = []

    def send(src, dst, ss, rs, device):
        copy = pltpu.make_async_remote_copy(
            src_ref=src, dst_ref=dst, send_sem=ss, recv_sem=rs, device_id=device, device_id_type=MESH
        )
        copy.start()
        return copy

    def pending(describe):
        sent.append(describe)

    def arrived(dst, rs):
        pltpu.make_async_remote_copy(
            src_ref=dst, dst_ref=dst, send_sem=rs, recv_sem=rs, device_id=SIB, device_id_type=MESH
        ).wait_recv()

    def quarter_of(d):
        return (y + d) % 4

    def piece(d, e, side):
        return pl.ds(pl.multiple_of(quarter_of(d) * quarter + (2 * side + e) * part, 16), part)

    def whole(d):
        return pl.ds(pl.multiple_of(quarter_of(d) * quarter, 16), quarter)

    def weight_x(m, d, e, device):
        rows = piece(d, e, core)
        send(w_any[m].at[rows], woth.at[m, rows], wps.at[m, d, e], wpr.at[m, d, e], device)
        pending(lambda: (w_any[m].at[piece(d, e, core)], wps.at[m, d, e]))

    def weight_first(m):
        for e in range(2):
            weight_x(m, 0, e, XD)
            weight_x(m, 2, e, XO)

    def weight_third(m):
        weight_x(m, 1, 0, XD)
        weight_x(m, 1, 1, XO)

    def weight_y(m, d, e, to_d, device):
        rows = piece(d, e, core)
        send(woth.at[m, rows], woth.at[m, rows], wps.at[m, to_d, e], wpr.at[m, to_d, e], device)
        pending(lambda: (woth.at[m, piece(d, e, core)], wps.at[m, to_d, e]))

    def weight_sib(m, d, e):
        rows = piece(d, e, core)
        arrived(woth.at[m, rows], wpr.at[m, d, e])
        send(woth.at[m, rows], woth.at[m, rows], wss.at[m, d, e], wsr.at[m, d, e], SIB)
        pending(lambda: (woth.at[m, piece(d, e, core)], wss.at[m, d, e]))

    def weight_on(m, e):
        weight_sib(m, 0, e)
        weight_sib(m, 2, e)
        if e == 0:
            weight_y(m, 0, 0, 3, YP)
            if not SHARE3[m]:
                weight_y(m, 0, 0, 1, YM)
        else:
            weight_y(m, 2, 1, 3, YM)
            if not SHARE3[m]:
                weight_y(m, 2, 1, 1, YP)

    def weight_rest(m):
        for d in (1, 3):
            for e in range(2):
                weight_sib(m, d, e)

    def weight_dot(m, d):
        for e in range(2):
            arrived(woth.at[m, piece(d, e, 1 - core)], wsr.at[m, d, e])
        lanes = pl.ds(pl.multiple_of((1 - c) * depth + quarter_of(d) * quarter, 128), quarter)
        raw[m] += jnp.dot(nrm[:, lanes], woth[m, whole(d), :], preferred_element_type=F32)

    mine = pl.ds(0, tok)
    other = pl.ds(tok, tok)

    def kv_out(i):
        src = stale_any.at[0, i]
        send(src, kvs.at[2, i, mine], kys.at[0, i], kyr.at[1, i], YP)
        send(src, kvs.at[1, i, mine], kys.at[1, i], kyr.at[0, i], YM)
        send(src, kvs.at[0, i, other], kss.at[0, i], ksr.at[0, i], SIB)
        pending(lambda: (stale_any.at[0, i], kys.at[0, i]))
        pending(lambda: (stale_any.at[0, i], kys.at[1, i]))
        pending(lambda: (stale_any.at[0, i], kss.at[0, i]))

    def kv_sib(slot, i):
        send(kvs.at[slot, i, mine], kvs.at[slot, i, other], kss.at[slot, i], ksr.at[slot, i], SIB)
        pending(lambda: (kvs.at[slot, i, pl.ds(0, tok)], kss.at[slot, i]))

    def kv_forward(i):
        for k, device in ((0, YM), (1, YP)):
            rows = pl.ds(k * half, half)
            arrived(kvs.at[1 + k, i, mine], kyr.at[k, i])
            send(kvs.at[1 + k, i, rows], kvs.at[3, i, rows], k3s.at[k, i], k3r.at[k, i], device)
            pending(lambda k=k: (kvs.at[1 + k, i, pl.ds(k * half, half)], k3s.at[k, i]))
            kv_sib(1 + k, i)

    def kv_last(i):
        for k in range(2):
            arrived(kvs.at[3, i, pl.ds(k * half, half)], k3r.at[k, i])
        kv_sib(3, i)

    def kv_ready(slot):
        for i in range(2):
            arrived(kvs.at[slot, i, other], ksr.at[slot, i])

    def squares_out(k, m):
        r = raw[m]
        column = jnp.broadcast_to(jnp.sum(r * r, axis=1, keepdims=True), (tok, 128))
        zs[k, 0] = jnp.zeros((8, 128), F32)
        for i in range(blocks):
            zs[k, 0, i : i + 1, :] = jnp.transpose(column[i * 128 : (i + 1) * 128])[:1, :]
        for d in range(1, n_head):
            send(zs.at[k, 0], zs.at[k, d], zss.at[k, d - 1], zsr.at[k, d - 1], ZS[d - 1])
            pending(lambda d=d: (zs.at[k, 0], zss.at[k, d - 1]))

    def norm_factor(k):
        total = zs[k, 0]
        for d in range(1, n_head):
            arrived(zs.at[k, d], zsr.at[k, d - 1])
            total = total + zs[k, d]
        return lax.rsqrt(total / columns_all + 1e-06)

    def column_of(rows, i):
        return jnp.transpose(jnp.broadcast_to(rows[i : i + 1, :], (128, 128)))

    def spread(s):
        rows = fac_rows[s]
        for i in range(blocks):
            fac[s, i * 128 : (i + 1) * 128, :] = column_of(rows, i)

    def head_gain(gain, j):
        return gain[j * 128 : (j + 1) * 128][None, :]

    def wide(v, keys):
        return jnp.concatenate([v] * (keys // 128), axis=1)

    tiles = 3 if tok % 48 == 0 else 1
    step = tok // tiles

    def attend(key_ref, value_ref):
        keys = key_ref.shape[0]
        for j in range(heads):
            lanes = slice(j * 128, (j + 1) * 128)
            for t in range(tiles):
                rows = slice(t * step, (t + 1) * step)
                value = value_ref[:, lanes]
                score = lax.dot_general(
                    qs[0, rows, lanes], key_ref[:, lanes], (((1,), (1,)), ((), ())), preferred_element_type=F32
                )
                score = score * wide(fac[0, rows, :], keys)
                before = top[j, rows, :]
                now = jnp.maximum(before, jnp.max(score, axis=1, keepdims=True))
                shrink = jnp.exp2(before - now)
                weight = jnp.exp2(score - wide(now, keys)).astype(BF16)
                added = jnp.dot(
                    weight, jnp.concatenate([value, jnp.ones_like(value)], axis=1), preferred_element_type=F32
                )
                acc[j, rows, :] = acc[j, rows, :] * wide(shrink, 256) + added
                top[j, rows, :] = now

    def partner_head(j):
        lanes = slice(j * 128, (j + 1) * 128)
        lane = lax.broadcasted_iota(jnp.int32, (step, 128), 1)
        for t in range(tiles):
            rows = slice(t * step, (t + 1) * step)
            query = qs[1, rows, lanes]
            factor = fac[1, rows, :]
            scores = [
                lax.dot_general(query, kvs[k, 0, :, lanes], (((1,), (1,)), ((), ())), preferred_element_type=F32)
                * wide(factor, 2 * tok)
                for k in range(4)
            ]
            highest = jnp.max(functools.reduce(jnp.maximum, scores), axis=1, keepdims=True)
            highest = jnp.broadcast_to(highest, (step, 128))
            summed = None
            for k in range(4):
                weight = jnp.exp2(scores[k] - wide(highest, 2 * tok)).astype(BF16)
                value = kvs[k, 1, :, lanes]
                added = jnp.dot(
                    weight, jnp.concatenate([value, jnp.ones_like(value)], axis=1), preferred_element_type=F32
                )
                summed = added if summed is None else summed + added
            total = summed[:, 128:]
            o_send[j, rows, :] = (summed[:, :128] / total).astype(BF16)
            lse[rows, :] = jnp.where(lane == j, highest + jnp.log2(total), lse[rows, :])

    weight_first(0)
    kv_out(0)
    weight_third(0)
    for m in (1, 2):
        weight_first(m)
        if SHARE3[m]:
            weight_third(m)

    loads[0].wait()

    def norm_rows(i, carry):
        rows = pl.ds(pl.multiple_of(i * 16, 16), 16)
        states = hid[rows, :].astype(F32)
        mean = jnp.mean(states, axis=1, keepdims=True)
        states = states - mean
        var = jnp.mean(states * states, axis=1, keepdims=True)
        nrm[rows, :] = (states * lax.rsqrt(var + 1e-06) * (1.0 + mod[1:2, :]) + mod[0:1, :]).astype(BF16)
        return carry

    lax.fori_loop(0, tok // 16, norm_rows, 0)

    for load in loads[1:4]:
        load.wait()
    own_lanes = pl.ds(pl.multiple_of(c * depth, 128), depth)

    def own_dot(m, carry):
        @pl.when(m == 1)
        def _():
            weight_on(0, 0)

        raw[m] = jnp.dot(nrm[:, own_lanes], wown[m], preferred_element_type=F32)
        return carry

    lax.fori_loop(0, 3, own_dot, 0)

    weight_on(0, 1)
    kv_out(1)
    top[...] = jnp.full_like(top, LOW)
    acc[...] = jnp.zeros_like(acc)
    lse[...] = jnp.zeros_like(lse)
    weight_dot(0, 0)
    weight_dot(0, 2)
    kv_forward(0)
    weight_rest(0)
    weight_dot(0, 1)
    weight_dot(0, 3)
    for j in range(heads):
        lanes = slice(j * 128, (j + 1) * 128)
        qs[0, :, lanes] = (raw[0, :, lanes] * head_gain(gain_q, j)).astype(BF16)
    send(qs.at[0], qs.at[1], qss.at[0], qsr.at[0], X2)
    pending(lambda: (qs.at[0], qss.at[0]))
    squares_out(0, 0)
    loads[4].wait()
    kv_ready(0)
    fac_rows[0] = norm_factor(0) * SCORE_SCALE
    send(fac_rows.at[0], fac_rows.at[1], qss.at[1], qsr.at[1], X2)
    pending(lambda: (fac_rows.at[0], qss.at[1]))
    spread(0)

    attend(kvs.at[0, 0, other], kvs.at[0, 1, other])
    kv_forward(1)

    def unit(i, carry):
        @pl.when(i == 0)
        def _():
            kv_ready(1)

        @pl.when(i == 1)
        def _():
            weight_on(1, 0)
            kv_ready(2)

        attend(kvs.at[i + 1, 0], kvs.at[i + 1, 1])
        return carry

    lax.fori_loop(0, 2, unit, 0)

    weight_on(1, 1)
    weight_dot(1, 0)
    weight_dot(1, 2)
    kv_last(0)
    kv_last(1)
    kv_ready(3)
    arrived(qs.at[1], qsr.at[0])
    arrived(fac_rows.at[1], qsr.at[1])
    spread(1)
    for j in range(heads):
        partner_head(j)
    for j in range(heads):
        send(o_send.at[j], o_recv.at[j], oss.at[j], osr.at[j], X2)
    lse_send[...] = jnp.transpose(lse[...])[:8, :]
    send(lse_send, lse_recv, oss.at[heads], osr.at[heads], X2)
    weight_on(2, 0)
    weight_on(2, 1)
    weight_rest(1)
    weight_dot(1, 1)
    weight_dot(1, 3)
    squares_out(1, 1)
    attend(kvs.at[3, 0], kvs.at[3, 1])
    for j in range(heads):
        pending(lambda j=j: (o_send.at[j], oss.at[j]))
    pending(lambda: (lse_send, oss.at[heads]))

    weight_dot(2, 0)
    weight_dot(2, 2)
    factors = norm_factor(1)
    for i in range(blocks):
        rows = slice(i * 128, (i + 1) * 128)
        factor = column_of(factors, i)
        for j in range(heads):
            lanes = slice(j * 128, (j + 1) * 128)
            fresh[0, 0, rows, lanes] = (raw[1, rows, lanes] * factor * head_gain(gain_k, j)).astype(BF16)
    results = [
        pltpu.make_async_copy(fresh.at[0, 0], fresh_out.at[0, 0], ld.at[0]),
        pltpu.make_async_copy(fresh.at[0, 1], fresh_out.at[0, 1], ld.at[1]),
        pltpu.make_async_copy(att, att_out, ld.at[2]),
    ]
    results[0].start()
    weight_rest(2)
    weight_dot(2, 1)
    weight_dot(2, 3)
    fresh[0, 1] = raw[2].astype(BF16)
    results[1].start()
    attend(fresh.at[0, 0], fresh.at[0, 1])

    for j in range(heads):
        arrived(o_recv.at[j], osr.at[j])
    arrived(lse_recv, osr.at[heads])
    far = jnp.transpose(jnp.concatenate([lse_recv[...]] * 16, axis=0))
    for j in range(heads):
        near = top[j]
        there = jnp.broadcast_to(far[:, j : j + 1], (tok, 128))
        highest = jnp.maximum(near, there)
        a = jnp.exp2(near - highest)
        b = jnp.exp2(there - highest)
        summed = acc[j, :, :128] * a + o_recv[j].astype(F32) * b
        att[0, :, j * 128 : (j + 1) * 128] = (summed / (acc[j, :, 128:] * a + b)).astype(BF16)
    results[2].start()

    for describe in sent:
        src, ss = describe()
        pltpu.make_async_remote_copy(
            src_ref=src, dst_ref=src, send_sem=ss, recv_sem=ss, device_id=SIB, device_id_type=MESH
        ).wait_send()
    for result in results:
        result.wait()


def hand_over(att_in, fresh_in, att_out, fresh_out, att, fresh, sem):
    tiles = [
        (fresh_in.at[0, 0], fresh.at[0, 0], fresh_out.at[0, 0]),
        (fresh_in.at[0, 1], fresh.at[0, 1], fresh_out.at[0, 1]),
        (att_in, att, att_out),
    ]
    come = [pltpu.make_async_copy(src, held, sem.at[0, i]) for i, (src, held, _) in enumerate(tiles)]
    go = [pltpu.make_async_copy(held, dst, sem.at[1, i]) for i, (_, held, dst) in enumerate(tiles)]
    for copy in come:
        copy.start()
    for first, second in zip(come, go):
        first.wait()
        second.start()
    for copy in go:
        copy.wait()


def local(n_head, hidden_states, modulation, w_query, w_key, w_value, query_gain, key_gain, stale_kv):
    tok = hidden_states.shape[1]
    depth, width = w_query.shape
    heads = width // HEAD_DIM
    hbm = pl.BlockSpec(memory_space=pl.ANY)
    vmem = pl.BlockSpec(memory_space=pltpu.VMEM)
    dma = pltpu.SemaphoreType.DMA
    peers = max(n_head - 1, 1)
    shapes = (
        jax.ShapeDtypeStruct((1, tok, width), BF16),
        jax.ShapeDtypeStruct((1, 2, tok, width), BF16),
    )
    results = pl.pallas_call(
        functools.partial(kernel, n_head, float(n_head * width)),
        out_shape=shapes,
        in_specs=[hbm, vmem, hbm, hbm, hbm, vmem, vmem, hbm],
        out_specs=(hbm, hbm),
        scratch_shapes=[
            pltpu.VMEM((1, tok, width), BF16),
            pltpu.VMEM((1, 2, tok, width), BF16),
            pltpu.VMEM((tok, 2 * depth), BF16),
            pltpu.VMEM((tok, 2 * depth), BF16),
            pltpu.VMEM((3, depth, width), BF16),
            pltpu.VMEM((3, depth, width), BF16),
            pltpu.VMEM((3, tok, width), F32),
            pltpu.VMEM((4, 2, 2 * tok, width), BF16),
            pltpu.VMEM((2, tok, width), BF16),
            pltpu.VMEM((2, tok, 128), F32),
            pltpu.VMEM((2, 8, 128), F32),
            pltpu.VMEM((heads, tok, 128), F32),
            pltpu.VMEM((heads, tok, 256), F32),
            pltpu.VMEM((heads, tok, 128), BF16),
            pltpu.VMEM((heads, tok, 128), BF16),
            pltpu.VMEM((tok, 128), F32),
            pltpu.VMEM((8, tok), F32),
            pltpu.VMEM((8, tok), F32),
            pltpu.VMEM((2, n_head, 8, 128), F32),
            dma((5,)),
            dma((3, 4, 2)), dma((3, 4, 2)), dma((3, 4, 2)), dma((3, 4, 2)),
            dma((2, 2)), dma((2, 2)), dma((2, 2)), dma((2, 2)), dma((4, 2)), dma((4, 2)),
            dma((2,)), dma((2,)), dma((heads + 1,)), dma((heads + 1,)), dma((2, peers)), dma((2, peers)),
        ],
        compiler_params=pltpu.CompilerParams(
            collective_id=0, has_side_effects=True, vmem_limit_bytes=60 * 2**20
        ),
    )(
        hidden_states, modulation, w_query, w_key, w_value,
        query_gain, key_gain, stale_kv,
    )
    return pl.pallas_call(
        hand_over,
        out_shape=shapes,
        in_specs=[hbm, hbm],
        out_specs=(hbm, hbm),
        scratch_shapes=[
            pltpu.VMEM((1, tok, width), BF16),
            pltpu.VMEM((1, 2, tok, width), BF16),
            dma((2, 3)),
        ],
    )(*results)


def solution(mesh):
    in_specs = (
        P("cfg", "patch", None),
        P(),
        P("cfg", "head"),
        P("cfg", "head"),
        P("cfg", "head"),
        P("head"),
        P("head"),
        P("cfg", None, "patch", "head"),
    )
    out_specs = (P("cfg", "patch", "head"), P("cfg", None, "patch", "head"))
    run = functools.partial(local, mesh.shape["head"])
    return jax.shard_map(run, mesh=mesh, in_specs=in_specs, out_specs=out_specs, check_vma=False)
```

```python
import functools

import jax
import jax.numpy as jnp
from jax import lax
from jax.experimental import pallas as pl
from jax.experimental.pallas import tpu as pltpu
from jax.sharding import PartitionSpec as P

HEAD_DIM = 128
SCORE_SCALE = 1.4426950408889634 / 128.0**0.5
LOW = -1e30
SHARE3 = (True, False, False)
MESH = pl.DeviceIdType.MESH
F32 = jnp.float32
BF16 = jnp.bfloat16


def kernel(
    n_head, columns_all,
    hid_any, mod, wq_any, wk_any, wv_any, gain_q, gain_k, stale_any,
    att_out, fresh_out,
    att, fresh, hid, nrm, wown, woth, raw, kvs, qs, top, acc, o_send, o_recv, lse, lse_send, lse_recv, zs,
    ld, wps, wpr, wss, wsr, kys, kyr, k3s, k3r, kss, ksr, qss, qsr, oss, osr, zss, zsr,
):
    tok = hid.shape[0]
    depth = wown.shape[1]
    width = wown.shape[2]
    heads = width // HEAD_DIM
    quarter = depth // 4
    part = quarter // 4
    half = tok // 2
    blocks = tok // 128

    c = lax.axis_index("cfg")
    p = lax.axis_index("patch")
    h = lax.axis_index("head")
    core = p % 2
    y = (p // 2) % 4
    xh = p // 8

    def at(xh_, y_, core_):
        return (xh_ * 4 + y_) * 2 + core_

    SIB = (c, at(xh, y, 1 - core), h)
    XD = (1 - c, p, h)
    XO = (1 - c, at(1 - xh, y, core), h)
    X2 = (c, at(1 - xh, y, core), h)
    YP = (c, at(xh, (y + 1) % 4, core), h)
    YM = (c, at(xh, (y + 3) % 4, core), h)
    ZS = [(c, p, (h + d) % n_head) for d in range(1, n_head)]
    w_any = (wq_any, wk_any, wv_any)

    loads = [
        pltpu.make_async_copy(hid_any.at[0], hid, ld.at[0]),
        pltpu.make_async_copy(wq_any, wown.at[0], ld.at[1]),
        pltpu.make_async_copy(wk_any, wown.at[1], ld.at[2]),
        pltpu.make_async_copy(wv_any, wown.at[2], ld.at[3]),
        pltpu.make_async_copy(stale_any.at[0], kvs.at[0, :, pl.ds(0, tok)], ld.at[4]),
    ]

    barrier = pltpu.get_barrier_semaphore()
    partners = [SIB, XD, XO, X2, YP, YM] + ZS
    for device in partners:
        pl.semaphore_signal(barrier, inc=1, device_id=device, device_id_type=MESH)
    for load in loads:
        load.start()
    pl.semaphore_wait(barrier, len(partners))

    sent = []

    def send(src, dst, ss, rs, device):
        copy = pltpu.make_async_remote_copy(
            src_ref=src, dst_ref=dst, send_sem=ss, recv_sem=rs, device_id=device, device_id_type=MESH
        )
        copy.start()
        return copy

    def pending(describe):
        sent.append(describe)

    def arrived(dst, rs):
        pltpu.make_async_remote_copy(
            src_ref=dst, dst_ref=dst, send_sem=rs, recv_sem=rs, device_id=SIB, device_id_type=MESH
        ).wait_recv()

    def quarter_of(d):
        return (y + d) % 4

    def piece(d, e, side):
        return pl.ds(pl.multiple_of(quarter_of(d) * quarter + (2 * side + e) * part, 16), part)

    def whole(d):
        return pl.ds(pl.multiple_of(quarter_of(d) * quarter, 16), quarter)

    def weight_x(m, d, e, device):
        rows = piece(d, e, core)
        send(w_any[m].at[rows], woth.at[m, rows], wps.at[m, d, e], wpr.at[m, d, e], device)
        pending(lambda: (w_any[m].at[piece(d, e, core)], wps.at[m, d, e]))

    def weight_first(m):
        for e in range(2):
            weight_x(m, 0, e, XD)
            weight_x(m, 2, e, XO)

    def weight_third(m):
        weight_x(m, 1, 0, XD)
        weight_x(m, 1, 1, XO)

    def weight_y(m, d, e, to_d, device):
        rows = piece(d, e, core)
        send(woth.at[m, rows], woth.at[m, rows], wps.at[m, to_d, e], wpr.at[m, to_d, e], device)
        pending(lambda: (woth.at[m, piece(d, e, core)], wps.at[m, to_d, e]))

    def weight_sib(m, d, e):
        rows = piece(d, e, core)
        arrived(woth.at[m, rows], wpr.at[m, d, e])
        send(woth.at[m, rows], woth.at[m, rows], wss.at[m, d, e], wsr.at[m, d, e], SIB)
        pending(lambda: (woth.at[m, piece(d, e, core)], wss.at[m, d, e]))

    def weight_on(m, e):
        weight_sib(m, 0, e)
        weight_sib(m, 2, e)
        if e == 0:
            weight_y(m, 0, 0, 3, YP)
            if not SHARE3[m]:
                weight_y(m, 0, 0, 1, YM)
        else:
            weight_y(m, 2, 1, 3, YM)
            if not SHARE3[m]:
                weight_y(m, 2, 1, 1, YP)

    def weight_rest(m):
        for d in (1, 3):
            for e in range(2):
                weight_sib(m, d, e)

    def weight_dot(m, d):
        for e in range(2):
            arrived(woth.at[m, piece(d, e, 1 - core)], wsr.at[m, d, e])
        lanes = pl.ds(pl.multiple_of((1 - c) * depth + quarter_of(d) * quarter, 128), quarter)
        raw[m] += jnp.dot(nrm[:, lanes], woth[m, whole(d), :], preferred_element_type=F32)

    mine = pl.ds(0, tok)
    other = pl.ds(tok, tok)

    def kv_out(i):
        src = stale_any.at[0, i]
        send(src, kvs.at[2, i, mine], kys.at[0, i], kyr.at[1, i], YP)
        send(src, kvs.at[1, i, mine], kys.at[1, i], kyr.at[0, i], YM)
        send(src, kvs.at[0, i, other], kss.at[0, i], ksr.at[0, i], SIB)
        pending(lambda: (stale_any.at[0, i], kys.at[0, i]))
        pending(lambda: (stale_any.at[0, i], kys.at[1, i]))
        pending(lambda: (stale_any.at[0, i], kss.at[0, i]))

    def kv_sib(slot, i):
        send(kvs.at[slot, i, mine], kvs.at[slot, i, other], kss.at[slot, i], ksr.at[slot, i], SIB)
        pending(lambda: (kvs.at[slot, i, pl.ds(0, tok)], kss.at[slot, i]))

    def kv_forward(i):
        for k, device in ((0, YM), (1, YP)):
            rows = pl.ds(k * half, half)
            arrived(kvs.at[1 + k, i, mine], kyr.at[k, i])
            send(kvs.at[1 + k, i, rows], kvs.at[3, i, rows], k3s.at[k, i], k3r.at[k, i], device)
            pending(lambda k=k: (kvs.at[1 + k, i, pl.ds(k * half, half)], k3s.at[k, i]))
            kv_sib(1 + k, i)

    def kv_last(i):
        for k in range(2):
            arrived(kvs.at[3, i, pl.ds(k * half, half)], k3r.at[k, i])
        kv_sib(3, i)

    def kv_ready(slot):
        for i in range(2):
            arrived(kvs.at[slot, i, other], ksr.at[slot, i])

    def squares_out(k, m):
        r = raw[m]
        column = jnp.broadcast_to(jnp.sum(r * r, axis=1, keepdims=True), (tok, 128))
        zs[k, 0] = jnp.zeros((8, 128), F32)
        for i in range(blocks):
            zs[k, 0, i : i + 1, :] = jnp.transpose(column[i * 128 : (i + 1) * 128])[:1, :]
        for d in range(1, n_head):
            send(zs.at[k, 0], zs.at[k, d], zss.at[k, d - 1], zsr.at[k, d - 1], ZS[d - 1])
            pending(lambda d=d: (zs.at[k, 0], zss.at[k, d - 1]))

    def norm_factor(k):
        total = zs[k, 0]
        for d in range(1, n_head):
            arrived(zs.at[k, d], zsr.at[k, d - 1])
            total = total + zs[k, d]
        return lax.rsqrt(total / columns_all + 1e-06)

    def column_of(rows, i):
        return jnp.transpose(jnp.broadcast_to(rows[i : i + 1, :], (128, 128)))

    def head_gain(gain, j):
        return gain[j * 128 : (j + 1) * 128][None, :]

    def normalise(k, m, gain, out):
        factors = norm_factor(k)
        for i in range(blocks):
            rows = slice(i * 128, (i + 1) * 128)
            factor = column_of(factors, i)
            for j in range(heads):
                lanes = slice(j * 128, (j + 1) * 128)
                out[rows, lanes] = (raw[m, rows, lanes] * factor * head_gain(gain, j)).astype(BF16)

    def wide(v, keys):
        return jnp.concatenate([v] * (keys // 128), axis=1)

    tiles = 3 if tok % 48 == 0 else 1
    step = tok // tiles

    def attend(key_ref, value_ref):
        keys = key_ref.shape[0]
        for j in range(heads):
            lanes = slice(j * 128, (j + 1) * 128)
            for t in range(tiles):
                rows = slice(t * step, (t + 1) * step)
                value = value_ref[:, lanes]
                score = lax.dot_general(
                    qs[0, rows, lanes], key_ref[:, lanes], (((1,), (1,)), ((), ())), preferred_element_type=F32
                )
                score = score * SCORE_SCALE
                before = top[j, rows, :]
                now = jnp.maximum(before, jnp.max(score, axis=1, keepdims=True))
                shrink = jnp.exp2(before - now)
                weight = jnp.exp2(score - wide(now, keys)).astype(BF16)
                added = jnp.dot(
                    weight, jnp.concatenate([value, jnp.ones_like(value)], axis=1), preferred_element_type=F32
                )
                acc[j, rows, :] = acc[j, rows, :] * wide(shrink, 256) + added
                top[j, rows, :] = now

    def partner_head(j):
        lanes = slice(j * 128, (j + 1) * 128)
        lane = lax.broadcasted_iota(jnp.int32, (step, 128), 1)
        for t in range(tiles):
            rows = slice(t * step, (t + 1) * step)
            query = qs[1, rows, lanes]
            scores = [
                lax.dot_general(query, kvs[k, 0, :, lanes], (((1,), (1,)), ((), ())), preferred_element_type=F32)
                * SCORE_SCALE
                for k in range(4)
            ]
            highest = jnp.max(functools.reduce(jnp.maximum, scores), axis=1, keepdims=True)
            highest = jnp.broadcast_to(highest, (step, 128))
            summed = None
            for k in range(4):
                weight = jnp.exp2(scores[k] - wide(highest, 2 * tok)).astype(BF16)
                value = kvs[k, 1, :, lanes]
                added = jnp.dot(
                    weight, jnp.concatenate([value, jnp.ones_like(value)], axis=1), preferred_element_type=F32
                )
                summed = added if summed is None else summed + added
            total = summed[:, 128:]
            o_send[j, rows, :] = (summed[:, :128] / total).astype(BF16)
            lse[rows, :] = jnp.where(lane == j, highest + jnp.log2(total), lse[rows, :])

    weight_first(0)
    kv_out(0)
    weight_third(0)
    for m in (1, 2):
        weight_first(m)
        if SHARE3[m]:
            weight_third(m)

    loads[0].wait()

    def norm_rows(i, carry):
        rows = pl.ds(pl.multiple_of(i * 16, 16), 16)
        states = hid[rows, :].astype(F32)
        mean = jnp.mean(states, axis=1, keepdims=True)
        states = states - mean
        var = jnp.mean(states * states, axis=1, keepdims=True)
        nrm[rows, :] = (states * lax.rsqrt(var + 1e-06) * (1.0 + mod[1:2, :]) + mod[0:1, :]).astype(BF16)
        return carry

    lax.fori_loop(0, tok // 16, norm_rows, 0)

    for load in loads[1:4]:
        load.wait()
    own_lanes = pl.ds(pl.multiple_of(c * depth, 128), depth)

    def own_dot(m, carry):
        @pl.when(m == 1)
        def _():
            weight_on(0, 0)

        raw[m] = jnp.dot(nrm[:, own_lanes], wown[m], preferred_element_type=F32)
        return carry

    lax.fori_loop(0, 3, own_dot, 0)

    weight_on(0, 1)
    kv_out(1)
    top[...] = jnp.full_like(top, LOW)
    acc[...] = jnp.zeros_like(acc)
    lse[...] = jnp.zeros_like(lse)
    weight_dot(0, 0)
    weight_dot(0, 2)
    kv_forward(0)
    weight_rest(0)
    weight_dot(0, 1)
    weight_dot(0, 3)
    squares_out(0, 0)
    loads[4].wait()
    kv_ready(0)
    normalise(0, 0, gain_q, qs.at[0])
    send(qs.at[0], qs.at[1], qss.at[0], qsr.at[0], X2)
    pending(lambda: (qs.at[0], qss.at[0]))

    attend(kvs.at[0, 0, other], kvs.at[0, 1, other])
    kv_forward(1)

    def unit(i, carry):
        @pl.when(i == 0)
        def _():
            kv_ready(1)

        @pl.when(i == 1)
        def _():
            weight_on(1, 0)
            kv_ready(2)

        attend(kvs.at[i + 1, 0], kvs.at[i + 1, 1])
        return carry

    lax.fori_loop(0, 2, unit, 0)

    weight_on(1, 1)
    weight_dot(1, 0)
    weight_dot(1, 2)
    kv_last(0)
    kv_last(1)
    kv_ready(3)
    arrived(qs.at[1], qsr.at[0])
    weight_on(2, 0)
    for j in range(min(3, heads)):
        partner_head(j)
    for j in range(min(3, heads)):
        send(o_send.at[j], o_recv.at[j], oss.at[j], osr.at[j], X2)
    weight_on(2, 1)
    for j in range(3, heads):
        partner_head(j)
    for j in range(3, heads):
        send(o_send.at[j], o_recv.at[j], oss.at[j], osr.at[j], X2)
    lse_send[...] = jnp.transpose(lse[...])[:8, :]
    send(lse_send, lse_recv, oss.at[heads], osr.at[heads], X2)
    weight_rest(1)
    weight_dot(1, 1)
    weight_dot(1, 3)
    squares_out(1, 1)
    attend(kvs.at[3, 0], kvs.at[3, 1])
    for j in range(heads):
        pending(lambda j=j: (o_send.at[j], oss.at[j]))
    pending(lambda: (lse_send, oss.at[heads]))

    weight_dot(2, 0)
    weight_dot(2, 2)
    normalise(1, 1, gain_k, fresh.at[0, 0])
    results = [
        pltpu.make_async_copy(fresh.at[0, 0], fresh_out.at[0, 0], ld.at[0]),
        pltpu.make_async_copy(fresh.at[0, 1], fresh_out.at[0, 1], ld.at[1]),
        pltpu.make_async_copy(att, att_out, ld.at[2]),
    ]
    results[0].start()
    weight_rest(2)
    weight_dot(2, 1)
    weight_dot(2, 3)
    fresh[0, 1] = raw[2].astype(BF16)
    results[1].start()
    attend(fresh.at[0, 0], fresh.at[0, 1])

    for j in range(heads):
        arrived(o_recv.at[j], osr.at[j])
    arrived(lse_recv, osr.at[heads])
    far = jnp.transpose(jnp.concatenate([lse_recv[...]] * 16, axis=0))
    for j in range(heads):
        near = top[j]
        there = jnp.broadcast_to(far[:, j : j + 1], (tok, 128))
        highest = jnp.maximum(near, there)
        a = jnp.exp2(near - highest)
        b = jnp.exp2(there - highest)
        summed = acc[j, :, :128] * a + o_recv[j].astype(F32) * b
        att[0, :, j * 128 : (j + 1) * 128] = (summed / (acc[j, :, 128:] * a + b)).astype(BF16)
    results[2].start()

    for describe in sent:
        src, ss = describe()
        pltpu.make_async_remote_copy(
            src_ref=src, dst_ref=src, send_sem=ss, recv_sem=ss, device_id=SIB, device_id_type=MESH
        ).wait_send()
    for result in results:
        result.wait()


def hand_over(att_in, fresh_in, att_out, fresh_out, att, fresh, sem):
    tiles = [
        (fresh_in.at[0, 0], fresh.at[0, 0], fresh_out.at[0, 0]),
        (fresh_in.at[0, 1], fresh.at[0, 1], fresh_out.at[0, 1]),
        (att_in, att, att_out),
    ]
    come = [pltpu.make_async_copy(src, held, sem.at[0, i]) for i, (src, held, _) in enumerate(tiles)]
    go = [pltpu.make_async_copy(held, dst, sem.at[1, i]) for i, (_, held, dst) in enumerate(tiles)]
    for copy in come:
        copy.start()
    for first, second in zip(come, go):
        first.wait()
        second.start()
    for copy in go:
        copy.wait()


def local(n_head, hidden_states, modulation, w_query, w_key, w_value, query_gain, key_gain, stale_kv):
    tok = hidden_states.shape[1]
    depth, width = w_query.shape
    heads = width // HEAD_DIM
    hbm = pl.BlockSpec(memory_space=pl.ANY)
    vmem = pl.BlockSpec(memory_space=pltpu.VMEM)
    dma = pltpu.SemaphoreType.DMA
    peers = max(n_head - 1, 1)
    shapes = (
        jax.ShapeDtypeStruct((1, tok, width), BF16),
        jax.ShapeDtypeStruct((1, 2, tok, width), BF16),
    )
    results = pl.pallas_call(
        functools.partial(kernel, n_head, float(n_head * width)),
        out_shape=shapes,
        in_specs=[hbm, vmem, hbm, hbm, hbm, vmem, vmem, hbm],
        out_specs=(hbm, hbm),
        scratch_shapes=[
            pltpu.VMEM((1, tok, width), BF16),
            pltpu.VMEM((1, 2, tok, width), BF16),
            pltpu.VMEM((tok, 2 * depth), BF16),
            pltpu.VMEM((tok, 2 * depth), BF16),
            pltpu.VMEM((3, depth, width), BF16),
            pltpu.VMEM((3, depth, width), BF16),
            pltpu.VMEM((3, tok, width), F32),
            pltpu.VMEM((4, 2, 2 * tok, width), BF16),
            pltpu.VMEM((2, tok, width), BF16),
            pltpu.VMEM((heads, tok, 128), F32),
            pltpu.VMEM((heads, tok, 256), F32),
            pltpu.VMEM((heads, tok, 128), BF16),
            pltpu.VMEM((heads, tok, 128), BF16),
            pltpu.VMEM((tok, 128), F32),
            pltpu.VMEM((8, tok), F32),
            pltpu.VMEM((8, tok), F32),
            pltpu.VMEM((2, n_head, 8, 128), F32),
            dma((5,)),
            dma((3, 4, 2)), dma((3, 4, 2)), dma((3, 4, 2)), dma((3, 4, 2)),
            dma((2, 2)), dma((2, 2)), dma((2, 2)), dma((2, 2)), dma((4, 2)), dma((4, 2)),
            dma((1,)), dma((1,)), dma((heads + 1,)), dma((heads + 1,)), dma((2, peers)), dma((2, peers)),
        ],
        compiler_params=pltpu.CompilerParams(
            collective_id=0, has_side_effects=True, vmem_limit_bytes=60 * 2**20
        ),
    )(
        hidden_states, modulation, w_query, w_key, w_value,
        query_gain, key_gain, stale_kv,
    )
    return pl.pallas_call(
        hand_over,
        out_shape=shapes,
        in_specs=[hbm, hbm],
        out_specs=(hbm, hbm),
        scratch_shapes=[
            pltpu.VMEM((1, tok, width), BF16),
            pltpu.VMEM((1, 2, tok, width), BF16),
            dma((2, 3)),
        ],
    )(*results)


def solution(mesh):
    in_specs = (
        P("cfg", "patch", None),
        P(),
        P("cfg", "head"),
        P("cfg", "head"),
        P("cfg", "head"),
        P("head"),
        P("head"),
        P("cfg", None, "patch", "head"),
    )
    out_specs = (P("cfg", "patch", "head"), P("cfg", None, "patch", "head"))
    run = functools.partial(local, mesh.shape["head"])
    return jax.shard_map(run, mesh=mesh, in_specs=in_specs, out_specs=out_specs, check_vma=False)
```

```python
import functools

import jax
import jax.numpy as jnp
from jax import lax
from jax.experimental import pallas as pl
from jax.experimental.pallas import tpu as pltpu
from jax.sharding import PartitionSpec as P

HEAD_DIM = 128
SCORE_SCALE = 1.4426950408889634 / 128.0**0.5
LOW = -1e30
SHARE3 = (True, False, False)
MESH = pl.DeviceIdType.MESH
F32 = jnp.float32
BF16 = jnp.bfloat16


def kernel(
    n_head, columns_all,
    hid_any, mod, wq_any, wk_any, wv_any, gain_q, gain_k, stale_any,
    att_out, fresh_out,
    att, fresh, hid, nrm, wown, woth, raw, kvs, qs, top, acc, o_send, o_recv, lse, lse_send, lse_recv, zs,
    ld, wps, wpr, wss, wsr, kys, kyr, k3s, k3r, kss, ksr, qss, qsr, oss, osr, zss, zsr,
):
    tok = hid.shape[0]
    depth = wown.shape[1]
    width = wown.shape[2]
    heads = width // HEAD_DIM
    quarter = depth // 4
    part = quarter // 4
    half = tok // 2
    blocks = tok // 128

    c = lax.axis_index("cfg")
    p = lax.axis_index("patch")
    h = lax.axis_index("head")
    core = p % 2
    y = (p // 2) % 4
    xh = p // 8

    def at(xh_, y_, core_):
        return (xh_ * 4 + y_) * 2 + core_

    SIB = (c, at(xh, y, 1 - core), h)
    XD = (1 - c, p, h)
    XO = (1 - c, at(1 - xh, y, core), h)
    X2 = (c, at(1 - xh, y, core), h)
    YP = (c, at(xh, (y + 1) % 4, core), h)
    YM = (c, at(xh, (y + 3) % 4, core), h)
    ZS = [(c, p, (h + d) % n_head) for d in range(1, n_head)]
    w_any = (wq_any, wk_any, wv_any)

    loads = [
        pltpu.make_async_copy(hid_any.at[0], hid, ld.at[0]),
        pltpu.make_async_copy(wq_any, wown.at[0], ld.at[1]),
        pltpu.make_async_copy(wk_any, wown.at[1], ld.at[2]),
        pltpu.make_async_copy(wv_any, wown.at[2], ld.at[3]),
        pltpu.make_async_copy(stale_any.at[0], kvs.at[0, :, pl.ds(0, tok)], ld.at[4]),
    ]

    barrier = pltpu.get_barrier_semaphore()
    partners = [SIB, XD, XO, X2, YP, YM] + ZS
    for device in partners:
        pl.semaphore_signal(barrier, inc=1, device_id=device, device_id_type=MESH)
    for load in loads:
        load.start()
    pl.semaphore_wait(barrier, len(partners))

    sent = []

    def send(src, dst, ss, rs, device):
        copy = pltpu.make_async_remote_copy(
            src_ref=src, dst_ref=dst, send_sem=ss, recv_sem=rs, device_id=device, device_id_type=MESH
        )
        copy.start()
        return copy

    def pending(describe):
        sent.append(describe)

    def arrived(dst, rs):
        pltpu.make_async_remote_copy(
            src_ref=dst, dst_ref=dst, send_sem=rs, recv_sem=rs, device_id=SIB, device_id_type=MESH
        ).wait_recv()

    def quarter_of(d):
        return (y + d) % 4

    def piece(d, e, side):
        return pl.ds(pl.multiple_of(quarter_of(d) * quarter + (2 * side + e) * part, 16), part)

    def whole(d):
        return pl.ds(pl.multiple_of(quarter_of(d) * quarter, 16), quarter)

    def weight_x(m, d, e, device):
        rows = piece(d, e, core)
        send(w_any[m].at[rows], woth.at[m, rows], wps.at[m, d, e], wpr.at[m, d, e], device)
        pending(lambda: (w_any[m].at[piece(d, e, core)], wps.at[m, d, e]))

    def weight_first(m):
        for e in range(2):
            weight_x(m, 0, e, XD)
            weight_x(m, 2, e, XO)

    def weight_third(m):
        weight_x(m, 1, 0, XD)
        weight_x(m, 1, 1, XO)

    def weight_y(m, d, e, to_d, device):
        rows = piece(d, e, core)
        send(woth.at[m, rows], woth.at[m, rows], wps.at[m, to_d, e], wpr.at[m, to_d, e], device)
        pending(lambda: (woth.at[m, piece(d, e, core)], wps.at[m, to_d, e]))

    def weight_sib(m, d, e):
        rows = piece(d, e, core)
        arrived(woth.at[m, rows], wpr.at[m, d, e])
        send(woth.at[m, rows], woth.at[m, rows], wss.at[m, d, e], wsr.at[m, d, e], SIB)
        pending(lambda: (woth.at[m, piece(d, e, core)], wss.at[m, d, e]))

    def weight_on(m, e):
        weight_sib(m, 0, e)
        weight_sib(m, 2, e)
        if e == 0:
            weight_y(m, 0, 0, 3, YP)
            if not SHARE3[m]:
                weight_y(m, 0, 0, 1, YM)
        else:
            weight_y(m, 2, 1, 3, YM)
            if not SHARE3[m]:
                weight_y(m, 2, 1, 1, YP)

    def weight_rest(m):
        for d in (1, 3):
            for e in range(2):
                weight_sib(m, d, e)

    def weight_dot(m, d):
        for e in range(2):
            arrived(woth.at[m, piece(d, e, 1 - core)], wsr.at[m, d, e])
        lanes = pl.ds(pl.multiple_of((1 - c) * depth + quarter_of(d) * quarter, 128), quarter)
        raw[m] += jnp.dot(nrm[:, lanes], woth[m, whole(d), :], preferred_element_type=F32)

    mine = pl.ds(0, tok)
    other = pl.ds(tok, tok)

    def kv_out(i):
        src = stale_any.at[0, i]
        send(src, kvs.at[2, i, mine], kys.at[0, i], kyr.at[1, i], YP)
        send(src, kvs.at[1, i, mine], kys.at[1, i], kyr.at[0, i], YM)
        send(src, kvs.at[0, i, other], kss.at[0, i], ksr.at[0, i], SIB)
        pending(lambda: (stale_any.at[0, i], kys.at[0, i]))
        pending(lambda: (stale_any.at[0, i], kys.at[1, i]))
        pending(lambda: (stale_any.at[0, i], kss.at[0, i]))

    def kv_sib(slot, i):
        send(kvs.at[slot, i, mine], kvs.at[slot, i, other], kss.at[slot, i], ksr.at[slot, i], SIB)
        pending(lambda: (kvs.at[slot, i, pl.ds(0, tok)], kss.at[slot, i]))

    def kv_forward(i):
        for k, device in ((0, YM), (1, YP)):
            rows = pl.ds(k * half, half)
            arrived(kvs.at[1 + k, i, mine], kyr.at[k, i])
            send(kvs.at[1 + k, i, rows], kvs.at[3, i, rows], k3s.at[k, i], k3r.at[k, i], device)
            pending(lambda k=k: (kvs.at[1 + k, i, pl.ds(k * half, half)], k3s.at[k, i]))
            kv_sib(1 + k, i)

    def kv_last(i):
        for k in range(2):
            arrived(kvs.at[3, i, pl.ds(k * half, half)], k3r.at[k, i])
        kv_sib(3, i)

    def kv_ready(slot):
        for i in range(2):
            arrived(kvs.at[slot, i, other], ksr.at[slot, i])

    def squares_out(k, m):
        r = raw[m]
        column = jnp.broadcast_to(jnp.sum(r * r, axis=1, keepdims=True), (tok, 128))
        zs[k, 0] = jnp.zeros((8, 128), F32)
        for i in range(blocks):
            zs[k, 0, i : i + 1, :] = jnp.transpose(column[i * 128 : (i + 1) * 128])[:1, :]
        for d in range(1, n_head):
            send(zs.at[k, 0], zs.at[k, d], zss.at[k, d - 1], zsr.at[k, d - 1], ZS[d - 1])
            pending(lambda d=d: (zs.at[k, 0], zss.at[k, d - 1]))

    def norm_factor(k):
        total = zs[k, 0]
        for d in range(1, n_head):
            arrived(zs.at[k, d], zsr.at[k, d - 1])
            total = total + zs[k, d]
        return lax.rsqrt(total / columns_all + 1e-06)

    def column_of(rows, i):
        return jnp.transpose(jnp.broadcast_to(rows[i : i + 1, :], (128, 128)))

    def head_gain(gain, j):
        return gain[j * 128 : (j + 1) * 128][None, :]

    def normalise(k, m, gain, out):
        factors = norm_factor(k)
        for i in range(blocks):
            rows = slice(i * 128, (i + 1) * 128)
            factor = column_of(factors, i)
            for j in range(heads):
                lanes = slice(j * 128, (j + 1) * 128)
                out[rows, lanes] = (raw[m, rows, lanes] * factor * head_gain(gain, j)).astype(BF16)

    def wide(v, keys):
        return jnp.concatenate([v] * (keys // 128), axis=1)

    tiles = 3 if tok % 48 == 0 else 1
    step = tok // tiles

    def attend(key_ref, value_ref):
        keys = key_ref.shape[0]
        for j in range(heads):
            lanes = slice(j * 128, (j + 1) * 128)
            for t in range(tiles):
                rows = slice(t * step, (t + 1) * step)
                value = value_ref[:, lanes]
                score = lax.dot_general(
                    qs[0, rows, lanes], key_ref[:, lanes], (((1,), (1,)), ((), ())), preferred_element_type=F32
                )
                score = score * SCORE_SCALE
                before = top[j, rows, :]
                now = jnp.maximum(before, jnp.max(score, axis=1, keepdims=True))
                shrink = jnp.exp2(before - now)
                weight = jnp.exp2(score - wide(now, keys)).astype(BF16)
                added = jnp.dot(
                    weight, jnp.concatenate([value, jnp.ones_like(value)], axis=1), preferred_element_type=F32
                )
                acc[j, rows, :] = acc[j, rows, :] * wide(shrink, 256) + added
                top[j, rows, :] = now

    def partner_head(j):
        lanes = slice(j * 128, (j + 1) * 128)
        lane = lax.broadcasted_iota(jnp.int32, (step, 128), 1)
        for t in range(tiles):
            rows = slice(t * step, (t + 1) * step)
            query = qs[1, rows, lanes]
            scores = [
                lax.dot_general(query, kvs[k, 0, :, lanes], (((1,), (1,)), ((), ())), preferred_element_type=F32)
                * SCORE_SCALE
                for k in range(4)
            ]
            highest = jnp.max(functools.reduce(jnp.maximum, scores), axis=1, keepdims=True)
            highest = jnp.broadcast_to(highest, (step, 128))
            summed = None
            for k in range(4):
                weight = jnp.exp2(scores[k] - wide(highest, 2 * tok)).astype(BF16)
                value = kvs[k, 1, :, lanes]
                added = jnp.dot(
                    weight, jnp.concatenate([value, jnp.ones_like(value)], axis=1), preferred_element_type=F32
                )
                summed = added if summed is None else summed + added
            total = summed[:, 128:]
            o_send[j, rows, :] = (summed[:, :128] / total).astype(BF16)
            lse[rows, :] = jnp.where(lane == j, highest + jnp.log2(total), lse[rows, :])

    weight_first(0)
    kv_out(0)
    weight_third(0)
    for m in (1, 2):
        weight_first(m)
        if SHARE3[m]:
            weight_third(m)

    loads[0].wait()

    def norm_rows(i, carry):
        rows = pl.ds(pl.multiple_of(i * 16, 16), 16)
        states = hid[rows, :].astype(F32)
        mean = jnp.mean(states, axis=1, keepdims=True)
        states = states - mean
        var = jnp.mean(states * states, axis=1, keepdims=True)
        nrm[rows, :] = (states * lax.rsqrt(var + 1e-06) * (1.0 + mod[1:2, :]) + mod[0:1, :]).astype(BF16)
        return carry

    lax.fori_loop(0, tok // 16, norm_rows, 0)

    for load in loads[1:4]:
        load.wait()
    own_lanes = pl.ds(pl.multiple_of(c * depth, 128), depth)

    def own_dot(m, carry):
        @pl.when(m == 1)
        def _():
            weight_on(0, 0)

        raw[m] = jnp.dot(nrm[:, own_lanes], wown[m], preferred_element_type=F32)
        return carry

    lax.fori_loop(0, 3, own_dot, 0)

    weight_on(0, 1)
    kv_out(1)
    top[...] = jnp.full_like(top, LOW)
    acc[...] = jnp.zeros_like(acc)
    lse[...] = jnp.zeros_like(lse)
    weight_dot(0, 0)
    weight_dot(0, 2)
    kv_forward(0)
    weight_rest(0)
    weight_dot(0, 1)
    weight_dot(0, 3)
    squares_out(0, 0)
    loads[4].wait()
    kv_ready(0)
    normalise(0, 0, gain_q, qs.at[0])
    send(qs.at[0], qs.at[1], qss.at[0], qsr.at[0], X2)
    pending(lambda: (qs.at[0], qss.at[0]))

    attend(kvs.at[0, 0, other], kvs.at[0, 1, other])
    kv_forward(1)

    def unit(i, carry):
        @pl.when(i == 0)
        def _():
            kv_ready(1)

        @pl.when(i == 1)
        def _():
            weight_on(1, 0)
            kv_ready(2)

        attend(kvs.at[i + 1, 0], kvs.at[i + 1, 1])
        return carry

    lax.fori_loop(0, 2, unit, 0)

    weight_on(1, 1)
    weight_dot(1, 0)
    weight_dot(1, 2)
    kv_last(0)
    kv_last(1)
    kv_ready(3)
    attend(kvs.at[3, 0], kvs.at[3, 1])
    arrived(qs.at[1], qsr.at[0])
    weight_on(2, 0)
    for j in range(min(3, heads)):
        partner_head(j)
    for j in range(min(3, heads)):
        send(o_send.at[j], o_recv.at[j], oss.at[j], osr.at[j], X2)
    weight_on(2, 1)
    for j in range(3, heads):
        partner_head(j)
    for j in range(3, heads):
        send(o_send.at[j], o_recv.at[j], oss.at[j], osr.at[j], X2)
    lse_send[...] = jnp.transpose(lse[...])[:8, :]
    send(lse_send, lse_recv, oss.at[heads], osr.at[heads], X2)
    weight_rest(1)
    weight_dot(1, 1)
    weight_dot(1, 3)
    squares_out(1, 1)
    for j in range(heads):
        pending(lambda j=j: (o_send.at[j], oss.at[j]))
    pending(lambda: (lse_send, oss.at[heads]))

    weight_dot(2, 0)
    weight_dot(2, 2)
    normalise(1, 1, gain_k, fresh.at[0, 0])
    results = [
        pltpu.make_async_copy(fresh.at[0, 0], fresh_out.at[0, 0], ld.at[0]),
        pltpu.make_async_copy(fresh.at[0, 1], fresh_out.at[0, 1], ld.at[1]),
        pltpu.make_async_copy(att, att_out, ld.at[2]),
    ]
    results[0].start()
    weight_rest(2)
    weight_dot(2, 1)
    weight_dot(2, 3)
    fresh[0, 1] = raw[2].astype(BF16)
    results[1].start()
    attend(fresh.at[0, 0], fresh.at[0, 1])

    for j in range(heads):
        arrived(o_recv.at[j], osr.at[j])
    arrived(lse_recv, osr.at[heads])
    far = jnp.transpose(jnp.concatenate([lse_recv[...]] * 16, axis=0))
    for j in range(heads):
        near = top[j]
        there = jnp.broadcast_to(far[:, j : j + 1], (tok, 128))
        highest = jnp.maximum(near, there)
        a = jnp.exp2(near - highest)
        b = jnp.exp2(there - highest)
        summed = acc[j, :, :128] * a + o_recv[j].astype(F32) * b
        att[0, :, j * 128 : (j + 1) * 128] = (summed / (acc[j, :, 128:] * a + b)).astype(BF16)
    results[2].start()

    for describe in sent:
        src, ss = describe()
        pltpu.make_async_remote_copy(
            src_ref=src, dst_ref=src, send_sem=ss, recv_sem=ss, device_id=SIB, device_id_type=MESH
        ).wait_send()
    for result in results:
        result.wait()


def hand_over(att_in, fresh_in, att_out, fresh_out, att, fresh, sem):
    tiles = [
        (fresh_in.at[0, 0], fresh.at[0, 0], fresh_out.at[0, 0]),
        (fresh_in.at[0, 1], fresh.at[0, 1], fresh_out.at[0, 1]),
        (att_in, att, att_out),
    ]
    come = [pltpu.make_async_copy(src, held, sem.at[0, i]) for i, (src, held, _) in enumerate(tiles)]
    go = [pltpu.make_async_copy(held, dst, sem.at[1, i]) for i, (_, held, dst) in enumerate(tiles)]
    for copy in come:
        copy.start()
    for first, second in zip(come, go):
        first.wait()
        second.start()
    for copy in go:
        copy.wait()


def local(n_head, hidden_states, modulation, w_query, w_key, w_value, query_gain, key_gain, stale_kv):
    tok = hidden_states.shape[1]
    depth, width = w_query.shape
    heads = width // HEAD_DIM
    hbm = pl.BlockSpec(memory_space=pl.ANY)
    vmem = pl.BlockSpec(memory_space=pltpu.VMEM)
    dma = pltpu.SemaphoreType.DMA
    peers = max(n_head - 1, 1)
    shapes = (
        jax.ShapeDtypeStruct((1, tok, width), BF16),
        jax.ShapeDtypeStruct((1, 2, tok, width), BF16),
    )
    results = pl.pallas_call(
        functools.partial(kernel, n_head, float(n_head * width)),
        out_shape=shapes,
        in_specs=[hbm, vmem, hbm, hbm, hbm, vmem, vmem, hbm],
        out_specs=(hbm, hbm),
        scratch_shapes=[
            pltpu.VMEM((1, tok, width), BF16),
            pltpu.VMEM((1, 2, tok, width), BF16),
            pltpu.VMEM((tok, 2 * depth), BF16),
            pltpu.VMEM((tok, 2 * depth), BF16),
            pltpu.VMEM((3, depth, width), BF16),
            pltpu.VMEM((3, depth, width), BF16),
            pltpu.VMEM((3, tok, width), F32),
            pltpu.VMEM((4, 2, 2 * tok, width), BF16),
            pltpu.VMEM((2, tok, width), BF16),
            pltpu.VMEM((heads, tok, 128), F32),
            pltpu.VMEM((heads, tok, 256), F32),
            pltpu.VMEM((heads, tok, 128), BF16),
            pltpu.VMEM((heads, tok, 128), BF16),
            pltpu.VMEM((tok, 128), F32),
            pltpu.VMEM((8, tok), F32),
            pltpu.VMEM((8, tok), F32),
            pltpu.VMEM((2, n_head, 8, 128), F32),
            dma((5,)),
            dma((3, 4, 2)), dma((3, 4, 2)), dma((3, 4, 2)), dma((3, 4, 2)),
            dma((2, 2)), dma((2, 2)), dma((2, 2)), dma((2, 2)), dma((4, 2)), dma((4, 2)),
            dma((1,)), dma((1,)), dma((heads + 1,)), dma((heads + 1,)), dma((2, peers)), dma((2, peers)),
        ],
        compiler_params=pltpu.CompilerParams(
            collective_id=0, has_side_effects=True, vmem_limit_bytes=60 * 2**20
        ),
    )(
        hidden_states, modulation, w_query, w_key, w_value,
        query_gain, key_gain, stale_kv,
    )
    return pl.pallas_call(
        hand_over,
        out_shape=shapes,
        in_specs=[hbm, hbm],
        out_specs=(hbm, hbm),
        scratch_shapes=[
            pltpu.VMEM((1, tok, width), BF16),
            pltpu.VMEM((1, 2, tok, width), BF16),
            dma((2, 3)),
        ],
    )(*results)


def solution(mesh):
    in_specs = (
        P("cfg", "patch", None),
        P(),
        P("cfg", "head"),
        P("cfg", "head"),
        P("cfg", "head"),
        P("head"),
        P("head"),
        P("cfg", None, "patch", "head"),
    )
    out_specs = (P("cfg", "patch", "head"), P("cfg", None, "patch", "head"))
    run = functools.partial(local, mesh.shape["head"])
    return jax.shard_map(run, mesh=mesh, in_specs=in_specs, out_specs=out_specs, check_vma=False)
```
